32 devices in a mesh: section: 4 (over x, core), blk: 8 (over z, y).
Axes of the slice: x: 2, y: 2, z: 4, core: 2. Of those that a mesh axis runs over, the one named last changes fastest.
Arguments:
- queries: bfloat16 [4, 1024, 4096], P('section', 'blk'), may hold values from -6 to 6
- key_heads: bfloat16 [4, 1024, 512], P('section', 'blk'), may hold values from -6 to 6
- value_per_head: bfloat16 [4, 1024, 512], P('section', 'blk'), may hold values from -6 to 6
- out_grads: bfloat16 [4, 1024, 4096], P('section', 'blk'), may hold values from -6 to 6
- segment_ids: int32 [4, 1024], P('section', 'blk'), may hold values from 0 to 63, never falling along the last dimension, each value on 1 to 64 neighbouring positions
- block_lists: int32 [4, 8, 4], P('section', 'blk'), may hold values from 0 to 7, as said below
- list_counts: int32 [4, 8], P('section', 'blk'), may hold values from 1 to 4, as said below
Outputs:
- grad_queries: bfloat16 [4, 1024, 4096], P('section', 'blk')
- grad_keys: bfloat16 [4, 1024, 512], P('section', 'blk')
- grad_values: bfloat16 [4, 1024, 512], P('section', 'blk')
The draws below stay inside these ranges and needn't reach their ends.
Inputs may be any that keep to these rules, and one draw needn't show every extreme that they name: `block_lists`: entry 0 of row b is b itself; for b >= 1 entry 1 is block 0; entries 2 to list_counts - 1 are distinct blocks between 1 and b - 1; entries from list_counts on repeat b. `list_counts`: at least 2 for every query block after the first; the last query block of every micro-batch uses all 4 slots.
All inputs are finite; a program needn't handle non-finite values.
Results may differ from the reference program's by a relative error of at most 0.0051.
Values may be sent and summed in bfloat16 or wider, within the bound.
No kernel may reach another device: no remote copies, remote signals or barrier semaphores. Data moves between devices by JAX's collectives and lax.ppermute only.
A program may use at most 64 MiB of HBM per device.

```python
import math
import jax
import jax.numpy as jnp
import numpy as np
from jax import lax

QUERY_HEADS = 32
KEY_VALUE_HEADS = 4
HEAD_SIZE = 128
MASK_BLOCK_SIZE = 128
LIST = 4
QUERY_BLOCKS = 8
MICRO_POSITIONS = 1024
MICRO_BATCHES = 4


def draw_queries(key, part):
    random_root_key = jax.random.fold_in(key, 1)
    value_tensor = jax.random.truncated_normal(random_root_key, -6.0, 6.0, (MICRO_BATCHES, MICRO_POSITIONS, QUERY_HEADS * HEAD_SIZE), jnp.float32)
    return value_tensor.astype(jnp.bfloat16)


def draw_key_heads(key, part):
    random_root_key = jax.random.fold_in(key, 2)
    value_tensor = jax.random.truncated_normal(random_root_key, -6.0, 6.0, (MICRO_BATCHES, MICRO_POSITIONS, KEY_VALUE_HEADS * HEAD_SIZE), jnp.float32)
    return value_tensor.astype(jnp.bfloat16)


def list_tables(key):
    table_key = jax.random.fold_in(key, 7)
    score_key, count_key = jax.random.split(table_key)
    column = jnp.arange(QUERY_BLOCKS, dtype=jnp.int32)
    raw_scores = jax.random.randint(score_key, (MICRO_BATCHES, QUERY_BLOCKS, QUERY_BLOCKS), 0, 1 << 20, jnp.int32) * QUERY_BLOCKS + column[None, None, :]
    row_block = column[None, :, None]
    valid = (column[None, None, :] >= 1) & (column[None, None, :] < row_block)
    masked = jnp.where(valid, raw_scores, (1 << 30) + column[None, None, :])
    order = jnp.argsort(masked, axis=-1, stable=True)[..., :LIST - 2].astype(jnp.int32)
    wanted = jax.random.randint(count_key, (MICRO_BATCHES, QUERY_BLOCKS), 2, LIST + 1, jnp.int32)
    query_block = column[None, :]
    upper = jnp.minimum(LIST, query_block + 1)
    lower = jnp.minimum(2, query_block + 1)
    counts = jnp.clip(wanted, lower, upper)
    counts = jnp.where(query_block == QUERY_BLOCKS - 1, upper, counts)
    own = jnp.broadcast_to(query_block[..., None], (MICRO_BATCHES, QUERY_BLOCKS, 1))
    entries = jnp.concatenate([own, jnp.zeros((MICRO_BATCHES, QUERY_BLOCKS, 1), jnp.int32), order], axis=-1)[..., :LIST]
    slots = jnp.arange(LIST, dtype=jnp.int32)
    entries = jnp.where(slots[None, None, :] < counts[..., None], entries, own)
    return (entries.astype(jnp.int32), counts.astype(jnp.int32))


def draw_block_lists(key, part):
    return list_tables(key)[0]


def draw_list_counts(key, part):
    return list_tables(key)[1]


def shard_levels(stream_key, extent, cuts, low, high):
    level = 1.0
    for position, parts in cuts:
        draws = jax.random.uniform(jax.random.fold_in(jax.random.fold_in(stream_key, 6), position), (parts,), jnp.float32, low / len(cuts), high / len(cuts))
        level = level * jnp.repeat(jnp.exp(draws), extent[position] // parts).reshape((-1,) + (1,) * (len(extent) - 1 - position))
    return level


def length_profile(number_of, total, most, slope):
    portions = [(1 << 20) // math.isqrt(standing ** slope) + 1 for standing in range(2, number_of + 1)]
    spare, given = total - most - (number_of - 1), [1] * (number_of - 1)
    while spare > 0:
        candidates = [i for i in range(number_of - 1) if given[i] < most]
        mass, budget = sum([portions[i] for i in candidates]), spare
        for i in candidates:
            addition = min(most - given[i], max(1, budget * portions[i] // mass), spare)
            given[i] = given[i] + addition
            spare = spare - addition
    return np.array([most] + given)


def uneven(stream_key, number_of, total, most, slope):
    if number_of == 2:
        one = jax.random.randint(stream_key, (), max(1, total - most), min(most, total - 1) + 1)
        return jnp.stack([one, total - one])
    lengths = jnp.asarray(length_profile(number_of, total, most, slope), jnp.int32)
    pairs = (number_of - 1) // 2
    giver, taker = lengths[1:1 + 2 * pairs:2], lengths[2:2 + 2 * pairs:2]
    room = jnp.minimum(giver - 1, most - taker)
    passed = jax.random.randint(jax.random.fold_in(stream_key, 1), (pairs,), 0, 1 << 20) % (room + 1)
    lengths = lengths.at[1:1 + 2 * pairs:2].set(giver - passed).at[2:2 + 2 * pairs:2].set(taker + passed)
    return lengths[jax.random.permutation(jax.random.fold_in(stream_key, 2), number_of)]


def gaussian(own_key, shape, scale, reach, shards=(), kind=jnp.bfloat16):
    values = jax.random.normal(own_key, shape, jnp.float32) * scale
    if len(shards) > 0:
        values = shard_levels(own_key, shape, shards, -0.22, 0.18) * values
    return jnp.clip(values, min=-reach, max=reach).astype(kind)


def setup_inputs(seed: int = 0) -> dict:
    keys = jax.random.split(jax.random.key(seed), 8)
    queries = draw_queries(jax.random.fold_in(keys[7], 71), 0)
    key_heads = draw_key_heads(jax.random.fold_in(keys[7], 71), 0)
    value_per_head = gaussian(keys[2], (MICRO_BATCHES, MICRO_POSITIONS, KEY_VALUE_HEADS * HEAD_SIZE), 1.0, 6.0, ((0, 4), (1, 8)))
    out_grads = gaussian(keys[3], (MICRO_BATCHES, MICRO_POSITIONS, QUERY_HEADS * HEAD_SIZE), 1.0, 6.0, ((0, 4), (1, 8)))
    segment_ids = jax.vmap(lambda own: jnp.searchsorted(jnp.cumsum(uneven(own, MICRO_POSITIONS // 16, MICRO_POSITIONS, 64, 2)), jnp.arange(MICRO_POSITIONS), side="right"))(jax.random.split(keys[4], MICRO_BATCHES)).reshape((MICRO_BATCHES, MICRO_POSITIONS)).astype(jnp.int32)
    block_lists = draw_block_lists(jax.random.fold_in(keys[7], 71), 0)
    list_counts = draw_list_counts(jax.random.fold_in(keys[7], 71), 0)
    return {"queries": queries, "key_heads": key_heads, "value_per_head": value_per_head, "out_grads": out_grads, "segment_ids": segment_ids, "block_lists": block_lists, "list_counts": list_counts}


NEG_FILL = -1e+30

def allowed_mask(block_ids, listed_count, query_block, query_segs):
    slot_ok = jnp.arange(LIST, dtype=jnp.int32) < listed_count
    own_block = block_ids == query_block
    positions = jnp.arange(MASK_BLOCK_SIZE, dtype=jnp.int32)
    causal = (positions[None, :] <= positions[:, None]) & (query_segs[None, :] == query_segs[:, None])
    earlier = block_ids < query_block
    return slot_ok[None, :, None] & jnp.where(own_block[None, :, None], causal[:, None, :], earlier[None, :, None])

def round_half(value_tensor):
    return lax.optimization_barrier(value_tensor.astype(jnp.bfloat16)).astype(jnp.float32)

def one_micro(operands):
    micro_queries, micro_keys, micro_values, micro_gradient, segs_m, lists_m, counts_m = operands
    heads_per_group = QUERY_HEADS // KEY_VALUE_HEADS
    scale_factor = 1.0 / math.sqrt(HEAD_SIZE)
    blocked_keys = micro_keys.reshape(QUERY_BLOCKS, MASK_BLOCK_SIZE, KEY_VALUE_HEADS, HEAD_SIZE)
    blocked_values = micro_values.reshape(QUERY_BLOCKS, MASK_BLOCK_SIZE, KEY_VALUE_HEADS, HEAD_SIZE)
    highest = lax.Precision.HIGHEST

    def step(running_total, inputs):
        query_block, block_ids, listed_count = inputs
        first_row_index = (query_block * MASK_BLOCK_SIZE).astype(jnp.int32)
        query_row_slice = lax.dynamic_slice_in_dim(micro_queries, first_row_index, MASK_BLOCK_SIZE, 0).astype(jnp.float32).reshape(MASK_BLOCK_SIZE, KEY_VALUE_HEADS, heads_per_group, HEAD_SIZE)
        gradient_row_slice = lax.dynamic_slice_in_dim(micro_gradient, first_row_index, MASK_BLOCK_SIZE, 0).astype(jnp.float32).reshape(MASK_BLOCK_SIZE, KEY_VALUE_HEADS, heads_per_group, HEAD_SIZE)
        query_segs = lax.dynamic_slice_in_dim(segs_m, first_row_index, MASK_BLOCK_SIZE, 0)
        allowed = allowed_mask(block_ids, listed_count, query_block, query_segs)[None, None]
        listed_k = blocked_keys[block_ids].astype(jnp.float32)
        listed_v = blocked_values[block_ids].astype(jnp.float32)
        scores = jnp.einsum('igrd,ljgd->grilj', query_row_slice, listed_k, precision=highest) * scale_factor
        scores = jnp.where(allowed, scores, NEG_FILL)
        largest = lax.optimization_barrier(jnp.max(scores, axis=(3, 4), keepdims=True))
        weights = jnp.where(allowed, jnp.exp(scores - largest), 0.0)
        probs_full = weights / lax.optimization_barrier(jnp.sum(weights, axis=(3, 4), keepdims=True))
        dprobs = jnp.einsum('igrd,ljgd->grilj', gradient_row_slice, listed_v, precision=highest)
        row_delta = lax.optimization_barrier(jnp.sum(probs_full * dprobs, axis=(3, 4), keepdims=True))
        dscores = round_half(probs_full * (dprobs - row_delta))
        probs_half = round_half(probs_full)
        query_grad = jnp.einsum('grilj,ljgd->igrd', dscores, listed_k, precision=highest) * scale_factor
        key_grad = jnp.einsum('grilj,igrd->ljgd', dscores, query_row_slice, precision=highest) * scale_factor
        value_grad = jnp.einsum('grilj,igrd->ljgd', probs_half, gradient_row_slice, precision=highest)
        running_total = (running_total[0].at[block_ids].add(key_grad), running_total[1].at[block_ids].add(value_grad))
        return (running_total, query_grad.reshape(MASK_BLOCK_SIZE, QUERY_HEADS * HEAD_SIZE).astype(jnp.bfloat16))
    zeroed_total = jnp.zeros((QUERY_BLOCKS, MASK_BLOCK_SIZE, KEY_VALUE_HEADS, HEAD_SIZE), jnp.float32)
    inputs = (jnp.arange(QUERY_BLOCKS, dtype=jnp.int32), lists_m, counts_m)
    running_total, query_gradient_rows = lax.scan(step, (zeroed_total, zeroed_total), inputs)
    return (query_gradient_rows.reshape(MICRO_POSITIONS, QUERY_HEADS * HEAD_SIZE), running_total[0].reshape(MICRO_POSITIONS, KEY_VALUE_HEADS * HEAD_SIZE).astype(jnp.bfloat16), running_total[1].reshape(MICRO_POSITIONS, KEY_VALUE_HEADS * HEAD_SIZE).astype(jnp.bfloat16))

def reference(queries, key_heads, value_per_head, out_grads, segment_ids, block_lists, list_counts):
    query_gradient_rows, key_grads, value_grads = lax.map(one_micro, (queries, key_heads, value_per_head, out_grads, segment_ids, block_lists, list_counts))
    return (jnp.roll(query_gradient_rows, -1, axis=0), jnp.roll(key_grads, -1, axis=0), jnp.roll(value_grads, -1, axis=0))
```

```python
import math

import jax
import jax.numpy as jnp
from jax import lax
from jax.experimental import pallas as pl
from jax.experimental.pallas import tpu as pltpu
from jax.sharding import PartitionSpec as P

QUERY_HEADS = 32
KEY_VALUE_HEADS = 4
HEAD_SIZE = 128
BLOCK = 128
LIST = 4
GROUP = QUERY_HEADS // KEY_VALUE_HEADS
HALF_KV = KEY_VALUE_HEADS // 2
HALF_Q = QUERY_HEADS // 2 * HEAD_SIZE
KV_COLS = HALF_KV * HEAD_SIZE
WIDE = GROUP * HEAD_SIZE
PAIR = 2 * HEAD_SIZE
MASKED = -1e30
NONE, WHOLE, CAUSAL = 0, 1, 2

SCALE = 1.0 / math.sqrt(HEAD_SIZE)
LOG2E = 1.0 / math.log(2.0)


def dot(a, b, contract):
    return lax.dot_general(
        a, b, ((contract[0], contract[1]), ((), ())), preferred_element_type=jnp.float32
    )


def attention_kernel(levels, *refs):
    place_ref, mode_ref, side_ref, segs_ref = refs[:4]
    query_ref, grad_ref, partner_ref = refs[4:7]
    held = refs[7 : 7 + levels]
    own_out, partner_out, here_ref = refs[7 + levels : 10 + levels]
    away_refs = refs[10 + levels : 9 + 2 * levels]
    kv, near, far, bias, probs, dscores, sums, arrived = refs[-8:]

    first_col = pl.multiple_of(side_ref[0] * HALF_Q, HALF_Q)
    copies = [
        pltpu.make_async_copy(held[j], kv.at[pl.ds(2 * j * BLOCK, 2 * BLOCK)], arrived.at[j])
        for j in range(levels)
    ]
    for which, ref in enumerate((query_ref, grad_ref)):
        copies.append(
            pltpu.make_async_copy(
                ref.at[:, pl.ds(first_col, HALF_Q)], near.at[which], arrived.at[levels + which]
            )
        )
    late = pltpu.make_async_copy(partner_ref, far, arrived.at[levels + 2])
    for copy in copies:
        copy.start()
    late.start()
    sums[...] = jnp.zeros_like(sums)

    key_at = lax.broadcasted_iota(jnp.int32, (BLOCK, BLOCK), 0)
    query_at = lax.broadcasted_iota(jnp.int32, (BLOCK, BLOCK), 1)
    for block in range(2):
        seg_of_query = jnp.broadcast_to(segs_ref[block : block + 1, :], (BLOCK, BLOCK))
        seg_of_key = seg_of_query.T
        causal = (key_at <= query_at) & (seg_of_key == seg_of_query)
        causal_bias = jnp.where(causal, 0.0, MASKED)
        for slot in range(LIST):
            mode = mode_ref[block * LIST + slot]
            flat = jnp.where(mode == WHOLE, 0.0, MASKED)
            bias[slot * BLOCK : (slot + 1) * BLOCK, :] = jnp.where(
                mode == CAUSAL, causal_bias, flat
            )
        if block == 0:
            for copy in copies:
                copy.wait()
        else:
            late.wait()

        def rows(which, head):
            if block == 0:
                return near[which, :, head * HEAD_SIZE : (head + 1) * HEAD_SIZE]
            start = which * HALF_Q + head * HEAD_SIZE
            return far[:, start : start + HEAD_SIZE]

        out = (own_out, partner_out)[block]
        places = [
            pl.ds(pl.multiple_of(place_ref[block * LIST + slot] * BLOCK, BLOCK), BLOCK)
            for slot in range(LIST)
        ]
        for group in range(HALF_KV):
            key_cols = slice(group * PAIR, group * PAIR + HEAD_SIZE)
            value_cols = slice(group * PAIR + HEAD_SIZE, (group + 1) * PAIR)
            heads = [group * GROUP + h for h in range(GROUP)]
            keys = jnp.concatenate([kv[at, key_cols] for at in places], axis=0)
            values = jnp.concatenate([kv[at, value_cols] for at in places], axis=0)
            for h in range(0, GROUP, 2):
                query = jnp.concatenate([rows(0, heads[h]), rows(0, heads[h + 1])], axis=0)
                grad = jnp.concatenate([rows(1, heads[h]), rows(1, heads[h + 1])], axis=0)
                scores = dot(keys, query, ((1,), (1,)))
                fill = jnp.concatenate([bias[...], bias[...]], axis=1)
                scores = scores * (SCALE * LOG2E) + fill
                weights = jnp.exp2(scores - jnp.max(scores, axis=0, keepdims=True))
                inverse = 1.0 / jnp.sum(weights, axis=0, keepdims=True)
                dprobs = dot(values, grad, ((1,), (1,)))
                full = weights * inverse
                delta = jnp.sum(full * dprobs, axis=0, keepdims=True)
                at = slice(h * BLOCK, (h + 2) * BLOCK)
                probs[:, at] = full.astype(jnp.bfloat16)
                dscores[:, at] = (full * (dprobs - delta)).astype(jnp.bfloat16)
            query_all = jnp.concatenate([rows(0, head) for head in heads], axis=0)
            grad_all = jnp.concatenate([rows(1, head) for head in heads], axis=0)
            key_terms = dot(dscores[...], query_all, ((1,), (0,))) * SCALE
            value_terms = dot(probs[...], grad_all, ((1,), (0,)))
            for slot in range(LIST):
                at = slice(slot * BLOCK, (slot + 1) * BLOCK)
                sums[places[slot], key_cols] += key_terms[at]
                sums[places[slot], value_cols] += value_terms[at]
            for h, head in enumerate(heads):
                query_grad = dot(dscores[:, h * BLOCK : (h + 1) * BLOCK], keys, ((0,), (0,)))
                out[:, head * HEAD_SIZE : (head + 1) * HEAD_SIZE] = (query_grad * SCALE).astype(
                    jnp.bfloat16
                )
    here_ref[...] = sums[: 2 * BLOCK]
    for j, ref in enumerate(away_refs):
        ref[...] = sums[2 * (j + 1) * BLOCK : 2 * (j + 2) * BLOCK].astype(ref.dtype)


def attention(levels, place, mode, side, segs, queries, grads, partner, held):
    smem = pl.BlockSpec(memory_space=pltpu.SMEM)
    vmem = pl.BlockSpec(memory_space=pltpu.VMEM)
    keys = LIST * BLOCK
    width = HALF_KV * PAIR
    outs = [
        jax.ShapeDtypeStruct((BLOCK, HALF_Q), jnp.bfloat16),
        jax.ShapeDtypeStruct((BLOCK, HALF_Q), jnp.bfloat16),
        jax.ShapeDtypeStruct((2 * BLOCK, width), jnp.float32),
    ]
    for j in range(1, levels):
        kind = jnp.float32 if 1 < j < levels - 1 else jnp.bfloat16
        outs.append(jax.ShapeDtypeStruct((2 * BLOCK, width), kind))
    return pl.pallas_call(
        lambda *refs: attention_kernel(levels, *refs),
        out_shape=outs,
        in_specs=[smem, smem, smem, vmem] + [pl.BlockSpec(memory_space=pl.ANY)] * (3 + levels),
        out_specs=[vmem] * len(outs),
        scratch_shapes=[
            pltpu.VMEM((2 * levels * BLOCK, width), jnp.bfloat16),
            pltpu.VMEM((2, BLOCK, HALF_Q), jnp.bfloat16),
            pltpu.VMEM((BLOCK, 2 * HALF_Q), jnp.bfloat16),
            pltpu.VMEM((keys, BLOCK), jnp.float32),
            pltpu.VMEM((keys, WIDE), jnp.bfloat16),
            pltpu.VMEM((keys, WIDE), jnp.bfloat16),
            pltpu.VMEM((2 * levels * BLOCK, width), jnp.float32),
            pltpu.SemaphoreType.DMA((levels + 3,)),
        ],
        compiler_params=pltpu.CompilerParams(vmem_limit_bytes=60 * 1024 * 1024),
        cost_estimate=pl.CostEstimate(
            flops=5 * 2 * keys * HEAD_SIZE * BLOCK * QUERY_HEADS,
            bytes_accessed=8 * 1024 * 1024,
            transcendentals=keys * BLOCK * QUERY_HEADS,
        ),
    )(place, mode, side, segs, queries, grads, partner, *held)


def per_device(
    queries, key_heads, value_per_head, out_grads, segment_ids, block_lists, list_counts
):
    sections = lax.axis_size("section")
    blocks = lax.axis_size("blk")
    levels = blocks // 2
    mine = lax.axis_index("blk")
    side = mine % 2
    level = mine // 2
    swap = [(i, i ^ 1) for i in range(blocks)]

    def back(value, moved):
        pairs = [
            (s * blocks + b, (s - 1) % sections * blocks + moved(b))
            for s in range(sections)
            for b in range(blocks)
            if moved(b) >= 0
        ]
        return lax.ppermute(value, ("section", "blk"), pairs)

    def columns(array, start, width):
        return lax.dynamic_slice_in_dim(array[0], start, width, 1)

    def heads_of(half):
        parts = []
        for g in range(HALF_KV):
            start = half * KV_COLS + g * HEAD_SIZE
            parts += [columns(a, start, HEAD_SIZE) for a in (key_heads, value_per_head)]
        return jnp.concatenate(parts, axis=1)

    facts = jnp.concatenate([segment_ids[0], block_lists[0, 0], list_counts[0]])[None]
    facts_got = lax.ppermute(facts, "blk", swap)
    other = lax.ppermute(heads_of(1 - side), "blk", swap)
    theirs = jnp.concatenate(
        [columns(a, (1 - side) * HALF_Q, HALF_Q) for a in (queries, out_grads)], axis=1
    )
    theirs, other, facts_got = lax.optimization_barrier((theirs, other, facts_got))
    partner = lax.ppermute(theirs, "blk", swap)
    held = [jnp.concatenate([heads_of(side), other], axis=0)]
    for hop in range(1, levels):
        pairs = [(i, i + 2 * hop) for i in range(blocks - 2 * hop)]
        held.append(lax.ppermute(held[0], "blk", pairs))

    facts = jnp.concatenate([facts, facts_got], axis=0)
    segs = facts[:, :BLOCK]
    lists = facts[:, BLOCK : BLOCK + LIST]
    counts = facts[:, BLOCK + LIST :]
    block = jnp.stack([mine, mine ^ 1])[:, None].astype(jnp.int32)
    listed = jnp.arange(LIST, dtype=jnp.int32)[None, :] < counts
    mode = jnp.where(lists == block, CAUSAL, jnp.where(lists < block, WHOLE, NONE))
    mode = jnp.where(listed, mode, NONE).astype(jnp.int32)
    place = 2 * (level - lists // 2) + (lists % 2 != side).astype(jnp.int32)
    place = jnp.where(mode == NONE, 0, place).astype(jnp.int32)

    own_out, partner_out, here, *away = attention(
        levels,
        place.reshape(-1),
        mode.reshape(-1),
        side.astype(jnp.int32)[None],
        segs,
        queries[0],
        out_grads[0],
        partner,
        held,
    )
    query_grads = (back(own_out, lambda b: b), back(partner_out, lambda b: b ^ 1))

    def down(terms, hop):
        return lax.ppermute(terms, "blk", [(i, i - 2 * hop) for i in range(2 * hop, blocks)])

    landed = []
    if levels > 1:
        landed.append(down(away[0], 1))
    if levels > 2:
        total = away[-1]
        for j in range(levels - 2, 1, -1):
            pairs = [(i, i - 2) for i in range(2 * (j + 1), blocks)]
            carried = lax.ppermute(total, "blk", pairs)
            total = (away[j - 1].astype(jnp.float32) + carried.astype(jnp.float32)).astype(jnp.bfloat16)
        landed.append(down(total, 2))
    landed, query_grads = lax.optimization_barrier((landed, query_grads))
    for terms in landed:
        here = here + terms.astype(jnp.float32)
    totals = here.astype(jnp.bfloat16)
    sums = [back(totals[:BLOCK], lambda b: b), back(totals[BLOCK:], lambda b: b ^ 1)]

    def ordered(a, b):
        return jnp.where(side == 0, jnp.concatenate([a, b], axis=1), jnp.concatenate([b, a], axis=1))

    grad_queries = ordered(*query_grads)

    def kind(total, which):
        starts = [g * PAIR + which * HEAD_SIZE for g in range(HALF_KV)]
        return jnp.concatenate([total[:, at : at + HEAD_SIZE] for at in starts], axis=1)

    grad_keys = ordered(kind(sums[0], 0), kind(sums[1], 0))
    grad_values = ordered(kind(sums[0], 1), kind(sums[1], 1))
    return (grad_queries[None], grad_keys[None], grad_values[None])


def solution(mesh):
    in_specs = (
        P("section", "blk", None),
        P("section", "blk", None),
        P("section", "blk", None),
        P("section", "blk", None),
        P("section", "blk"),
        P("section", "blk", None),
        P("section", "blk"),
    )
    out_specs = (P("section", "blk", None), P("section", "blk", None), P("section", "blk", None))
    return jax.shard_map(
        per_device, mesh=mesh, in_specs=in_specs, out_specs=out_specs, check_vma=False
    )
```

```python
import math

import jax
import jax.numpy as jnp
from jax import lax
from jax.experimental import pallas as pl
from jax.experimental.pallas import tpu as pltpu
from jax.sharding import PartitionSpec as P

QUERY_HEADS = 32
KEY_VALUE_HEADS = 4
HEAD_SIZE = 128
BLOCK = 128
LIST = 4
GROUP = QUERY_HEADS // KEY_VALUE_HEADS
HALF_KV = KEY_VALUE_HEADS // 2
HALF_Q = QUERY_HEADS // 2 * HEAD_SIZE
KV_COLS = HALF_KV * HEAD_SIZE
WIDE = GROUP * HEAD_SIZE
PAIR = 2 * HEAD_SIZE
MASKED = -1e30
NONE, WHOLE, CAUSAL = 0, 1, 2

SCALE = 1.0 / math.sqrt(HEAD_SIZE)
FACTOR = SCALE / math.log(2.0)


def dot(a, b, contract):
    return lax.dot_general(
        a, b, ((contract[0], contract[1]), ((), ())), preferred_element_type=jnp.float32
    )


def attention_kernel(levels, *refs):
    place_ref, mode_ref, side_ref, segs_ref = refs[:4]
    query_ref, grad_ref, partner_ref = refs[4:7]
    held = refs[7 : 7 + levels][::-1]
    outs = refs[7 + levels : 9 + levels]
    term_refs = refs[9 + levels : 9 + 2 * levels]
    scratch = refs[9 + 2 * levels :]
    rows_of = [pl.ds(2 * j * BLOCK, 2 * BLOCK) for j in range(levels - 1)]
    rows_of.append(pl.ds(pl.multiple_of(2 * side_ref[1] * BLOCK, 2 * BLOCK), 2 * BLOCK))
    kv, rows_in, rows_out, bias, probs, dscores, sums = scratch[:7]
    terms = scratch[7 : 7 + levels]
    arrived, left = scratch[-2:]

    first_col = side_ref[0] * HALF_Q
    arrivals = []
    for group in range(HALF_KV):
        at = pl.ds(group * PAIR, PAIR)
        copies = [
            pltpu.make_async_copy(
                held[j].at[:, at],
                kv.at[pl.ds(2 * j * BLOCK, 2 * BLOCK), at],
                arrived.at[group, j],
            )
            for j in range(levels)
        ]
        blocks = []
        for block in range(2):
            pair = []
            for which, ref in enumerate((query_ref, grad_ref)):
                if block == 0:
                    start = pl.multiple_of(first_col + group * WIDE, WIDE)
                    source = ref.at[:, pl.ds(start, WIDE)]
                else:
                    source = partner_ref.at[:, pl.ds(which * HALF_Q + group * WIDE, WIDE)]
                pair.append(
                    pltpu.make_async_copy(
                        source,
                        rows_in.at[block, which, :, pl.ds(group * WIDE, WIDE)],
                        arrived.at[group, levels + 2 * block + which],
                    )
                )
            blocks.append(pair)
        arrivals.append((copies, blocks))
    for copies, blocks in arrivals:
        for copy in copies + blocks[0] + blocks[1]:
            copy.start()
    sums[...] = jnp.zeros_like(sums)

    key_at = lax.broadcasted_iota(jnp.int32, (BLOCK, BLOCK), 0)
    query_at = lax.broadcasted_iota(jnp.int32, (BLOCK, BLOCK), 1)
    shifts = []
    places = []
    for block in range(2):
        seg_of_query = jnp.broadcast_to(segs_ref[block : block + 1, :], (BLOCK, BLOCK))
        causal = (key_at <= query_at) & (seg_of_query.T == seg_of_query)
        mode = mode_ref[block * LIST]
        bias[block] = jnp.where((mode == CAUSAL) & causal, 0.0, MASKED)
        shifts.append(
            [
                jnp.where(mode_ref[block * LIST + slot] == WHOLE, 0.0, -MASKED)
                for slot in range(1, LIST)
            ]
        )
        places.append(
            [
                pl.ds(pl.multiple_of(place_ref[block * LIST + slot] * BLOCK, BLOCK), BLOCK)
                for slot in range(LIST)
            ]
        )

    departures = []

    def send(source, target):
        copy = pltpu.make_async_copy(source, target, left.at[len(departures)])
        copy.start()
        departures.append(copy)

    for group in range(HALF_KV):
        copies, blocks = arrivals[group]
        for copy in copies:
            copy.wait()
        key_cols = slice(group * PAIR, group * PAIR + HEAD_SIZE)
        value_cols = slice(group * PAIR + HEAD_SIZE, (group + 1) * PAIR)
        heads = [group * GROUP + h for h in range(GROUP)]
        for block in range(2):
            for copy in blocks[block]:
                copy.wait()

            def rows(which, head):
                return rows_in[block, which, :, head * HEAD_SIZE : (head + 1) * HEAD_SIZE]

            keys = jnp.concatenate([kv[at, key_cols] for at in places[block]], axis=0)
            values = jnp.concatenate([kv[at, value_cols] for at in places[block]], axis=0)
            shift = shifts[block]

            def products(h):
                query = jnp.concatenate([rows(0, heads[h]), rows(0, heads[h + 1])], axis=0)
                grad = jnp.concatenate([rows(1, heads[h]), rows(1, heads[h + 1])], axis=0)
                each = [slice(slot * BLOCK, (slot + 1) * BLOCK) for slot in range(LIST)]
                return (
                    [dot(keys[at], query, ((1,), (1,))) for at in each],
                    [dot(values[at], grad, ((1,), (1,))) for at in each],
                )

            for h in range(0, GROUP, 2):
                scores, dprobs = products(h)
                parts = list(scores)
                parts[0] = parts[0] + jnp.concatenate([bias[block], bias[block]], axis=1)

                def fold(value, by):
                    return by(value.reshape(BLOCK // 8, 8, 2 * BLOCK), axis=0)

                peak = fold(parts[0], jnp.max)
                for slot in range(1, LIST):
                    peak = jnp.maximum(peak, fold(parts[slot], jnp.max) - shift[slot - 1])
                peak = jnp.max(peak, axis=0, keepdims=True) * FACTOR
                peaks = [peak] + [peak + shift[slot - 1] for slot in range(1, LIST)]
                total = jnp.zeros((8, 2 * BLOCK), jnp.float32)
                mixed = jnp.zeros((8, 2 * BLOCK), jnp.float32)
                weights = []
                for slot in range(LIST):
                    weight = jnp.exp2(parts[slot] * FACTOR - peaks[slot])
                    total = total + fold(weight, jnp.sum)
                    mixed = mixed + fold(weight * dprobs[slot], jnp.sum)
                    weights.append(weight)
                inverse = 1.0 / jnp.sum(total, axis=0, keepdims=True)
                delta = jnp.sum(mixed, axis=0, keepdims=True) * inverse
                at = slice(h * BLOCK, (h + 2) * BLOCK)
                for slot in range(LIST):
                    full = weights[slot] * inverse
                    down = slice(slot * BLOCK, (slot + 1) * BLOCK)
                    probs[down, at] = full.astype(jnp.bfloat16)
                    dscores[down, at] = (full * (dprobs[slot] - delta)).astype(jnp.bfloat16)
            query_all = jnp.concatenate([rows(0, head) for head in heads], axis=0)
            grad_all = jnp.concatenate([rows(1, head) for head in heads], axis=0)
            query_grad = dot(dscores[...], keys, ((0,), (0,))) * SCALE
            for h, head in enumerate(heads):
                rows_out[block, :, head * HEAD_SIZE : (head + 1) * HEAD_SIZE] = query_grad[
                    h * BLOCK : (h + 1) * BLOCK
                ].astype(jnp.bfloat16)
            wide = pl.ds(group * WIDE, WIDE)
            send(rows_out.at[block, :, wide], outs[block].at[:, wide])
            key_terms = dot(dscores[...], query_all, ((1,), (0,))) * SCALE
            value_terms = dot(probs[...], grad_all, ((1,), (0,)))
            for slot in range(LIST):
                at = slice(slot * BLOCK, (slot + 1) * BLOCK)
                sums[places[block][slot], key_cols] += key_terms[at]
                sums[places[block][slot], value_cols] += value_terms[at]
        cols = slice(group * PAIR, (group + 1) * PAIR)
        for j in range(levels):
            terms[j][:, cols] = sums[rows_of[j], cols].astype(terms[j].dtype)
            cut = pl.ds(group * PAIR, PAIR)
            send(terms[j].at[:, cut], term_refs[j].at[:, cut])
    for copy in departures:
        copy.wait()


def attention(levels, place, mode, side, segs, queries, grads, partner, held):
    smem = pl.BlockSpec(memory_space=pltpu.SMEM)
    anywhere = pl.BlockSpec(memory_space=pl.ANY)
    keys = LIST * BLOCK
    width = HALF_KV * PAIR
    outs = [jax.ShapeDtypeStruct((BLOCK, HALF_Q), jnp.bfloat16)] * 2
    terms = [
        jax.ShapeDtypeStruct(
            (2 * BLOCK, width), jnp.bfloat16 if j in (1, levels - 1) else jnp.float32
        )
        for j in range(levels)
    ]
    return pl.pallas_call(
        lambda *refs: attention_kernel(levels, *refs),
        out_shape=outs + terms,
        in_specs=[smem, smem, smem, pl.BlockSpec(memory_space=pltpu.VMEM)]
        + [anywhere] * (3 + levels),
        out_specs=[anywhere] * (2 + levels),
        scratch_shapes=[
            pltpu.VMEM((2 * levels * BLOCK, width), jnp.bfloat16),
            pltpu.VMEM((2, 2, BLOCK, HALF_Q), jnp.bfloat16),
            pltpu.VMEM((2, BLOCK, HALF_Q), jnp.bfloat16),
            pltpu.VMEM((2, BLOCK, BLOCK), jnp.float32),
            pltpu.VMEM((keys, WIDE), jnp.bfloat16),
            pltpu.VMEM((keys, WIDE), jnp.bfloat16),
            pltpu.VMEM((2 * levels * BLOCK, width), jnp.float32),
        ]
        + [pltpu.VMEM(term.shape, term.dtype) for term in terms]
        + [
            pltpu.SemaphoreType.DMA((HALF_KV, levels + 4)),
            pltpu.SemaphoreType.DMA((HALF_KV * (levels + 2),)),
        ],
        compiler_params=pltpu.CompilerParams(vmem_limit_bytes=60 * 1024 * 1024),
        cost_estimate=pl.CostEstimate(
            flops=5 * 2 * keys * HEAD_SIZE * BLOCK * QUERY_HEADS,
            bytes_accessed=8 * 1024 * 1024,
            transcendentals=keys * BLOCK * QUERY_HEADS,
        ),
    )(place, mode, side, segs, queries, grads, partner, *held[::-1])


def per_device(
    queries, key_heads, value_per_head, out_grads, segment_ids, block_lists, list_counts
):
    sections = lax.axis_size("section")
    blocks = lax.axis_size("blk")
    levels = blocks // 2
    mine = lax.axis_index("blk")
    side = mine % 2
    level = mine // 2
    swap = [(i, i ^ 1) for i in range(blocks)]

    def back(value, moved):
        pairs = [
            (s * blocks + b, (s - 1) % sections * blocks + moved(b))
            for s in range(sections)
            for b in range(blocks)
            if moved(b) >= 0
        ]
        return lax.ppermute(value, ("section", "blk"), pairs)

    def columns(array, start, width):
        return lax.dynamic_slice_in_dim(array[0], start, width, 1)

    def heads_of(half):
        parts = []
        for g in range(HALF_KV):
            start = half * KV_COLS + g * HEAD_SIZE
            parts += [columns(a, start, HEAD_SIZE) for a in (key_heads, value_per_head)]
        return jnp.concatenate(parts, axis=1)

    facts = jnp.concatenate([segment_ids[0], block_lists[0, 0], list_counts[0]])[None]
    facts_got = lax.ppermute(facts, "blk", swap)
    other = lax.ppermute(heads_of(1 - side), "blk", swap)
    theirs = jnp.concatenate(
        [columns(a, (1 - side) * HALF_Q, HALF_Q) for a in (queries, out_grads)], axis=1
    )
    theirs, other, facts_got = lax.optimization_barrier((theirs, other, facts_got))
    partner = lax.ppermute(theirs, "blk", swap)
    held = [jnp.concatenate([heads_of(side), other], axis=0)]
    for hop in range(1, levels):
        pairs = [(i, i + 2 * hop) for i in range(blocks - 2 * hop)]
        held.append(lax.ppermute(held[0], "blk", pairs))

    facts = jnp.concatenate([facts, facts_got], axis=0)
    segs = facts[:, :BLOCK]
    lists = facts[:, BLOCK : BLOCK + LIST]
    counts = facts[:, BLOCK + LIST :]
    block = jnp.stack([mine, mine ^ 1])[:, None].astype(jnp.int32)
    listed = jnp.arange(LIST, dtype=jnp.int32)[None, :] < counts
    mode = jnp.where(lists == block, CAUSAL, jnp.where(lists < block, WHOLE, NONE))
    mode = jnp.where(listed, mode, NONE).astype(jnp.int32)
    place = 2 * (level - lists // 2) + (lists % 2 != side).astype(jnp.int32)
    place = jnp.where(mode == NONE, 0, place).astype(jnp.int32)

    top = levels - 1
    own_out, partner_out, here, near, *between, first = attention(
        levels,
        place.reshape(-1),
        mode.reshape(-1),
        jnp.stack([side, jnp.where(level == top, top, 1)]).astype(jnp.int32),
        segs,
        queries[0],
        out_grads[0],
        partner,
        held,
    )

    def down(terms, hop, lowest):
        pairs = [(i, i - 2 * hop) for i in range(2 * lowest, blocks)]
        return lax.ppermute(terms, "blk", pairs)

    landed = down(first, 1, 1)
    query_grads = (back(own_out, lambda b: b), back(partner_out, lambda b: b ^ 1))
    carried = landed
    for j in range(top - 1, 1, -1):
        total = between[j - 2] + carried.astype(jnp.float32)
        total = total.astype(jnp.bfloat16)
        carried = down(total, 1, j) if j > 2 else down(total, 2, 2)
    here = here + jnp.where(level == top - 1, 0.0, landed.astype(jnp.float32))
    near, here = lax.optimization_barrier((near, here))
    rest = down(near, 1, top)
    rest, query_grads, carried = lax.optimization_barrier((rest, query_grads, carried))
    totals = (here + carried.astype(jnp.float32) + rest.astype(jnp.float32)).astype(jnp.bfloat16)
    sums = [back(totals[:BLOCK], lambda b: b), back(totals[BLOCK:], lambda b: b ^ 1)]

    def ordered(a, b):
        return jnp.where(side == 0, jnp.concatenate([a, b], axis=1), jnp.concatenate([b, a], axis=1))

    grad_queries = ordered(*query_grads)

    def kind(total, which):
        starts = [g * PAIR + which * HEAD_SIZE for g in range(HALF_KV)]
        return jnp.concatenate([total[:, at : at + HEAD_SIZE] for at in starts], axis=1)

    grad_keys = ordered(kind(sums[0], 0), kind(sums[1], 0))
    grad_values = ordered(kind(sums[0], 1), kind(sums[1], 1))
    return (grad_queries[None], grad_keys[None], grad_values[None])


def solution(mesh):
    in_specs = (
        P("section", "blk", None),
        P("section", "blk", None),
        P("section", "blk", None),
        P("section", "blk", None),
        P("section", "blk"),
        P("section", "blk", None),
        P("section", "blk"),
    )
    out_specs = (P("section", "blk", None), P("section", "blk", None), P("section", "blk", None))
    return jax.shard_map(
        per_device, mesh=mesh, in_specs=in_specs, out_specs=out_specs, check_vma=False
    )
```

```python
import math

import jax
import jax.numpy as jnp
from jax import lax
from jax.experimental import pallas as pl
from jax.experimental.pallas import tpu as pltpu
from jax.sharding import PartitionSpec as P

QUERY_HEADS = 32
KEY_VALUE_HEADS = 4
HEAD_SIZE = 128
BLOCK = 128
LIST = 4
GROUP = QUERY_HEADS // KEY_VALUE_HEADS
HALF_KV = KEY_VALUE_HEADS // 2
HALF_Q = QUERY_HEADS // 2 * HEAD_SIZE
KV_COLS = HALF_KV * HEAD_SIZE
WIDE = GROUP * HEAD_SIZE
PAIR = 2 * HEAD_SIZE
MASKED = -1e30

SCALE = 1.0 / math.sqrt(HEAD_SIZE)
FACTOR = SCALE / math.log(2.0)


def dot(a, b, contract):
    return lax.dot_general(
        a, b, ((contract[0], contract[1]), ((), ())), preferred_element_type=jnp.float32
    )


def attention_kernel(levels, *refs):
    list_ref, count_ref, where_ref, segs_ref, told_ref = refs[:5]
    refs = refs[1:]
    query_ref, grad_ref, partner_ref = refs[4:7]
    held = refs[7 : 7 + levels][::-1]
    outs = refs[7 + levels : 9 + levels]
    term_refs = refs[9 + levels : 9 + 2 * levels]
    scratch = refs[9 + 2 * levels :]
    rows_of = [pl.ds(2 * j * BLOCK, 2 * BLOCK) for j in range(levels - 1)]
    rows_of.append(pl.ds(pl.multiple_of(2 * where_ref[1] * BLOCK, 2 * BLOCK), 2 * BLOCK))
    kv, rows_in, rows_out, bias, probs, dscores, sums = scratch[:7]
    terms = scratch[7 : 7 + levels]
    arrived, left = scratch[-2:]

    mine = where_ref[0]
    side = mine & 1
    first_col = side * HALF_Q
    arrivals = []
    for group in range(HALF_KV):
        at = pl.ds(group * PAIR, PAIR)
        copies = [
            pltpu.make_async_copy(
                held[j].at[:, at],
                kv.at[pl.ds(2 * j * BLOCK, 2 * BLOCK), at],
                arrived.at[group, j],
            )
            for j in range(levels)
        ]
        blocks = []
        for block in range(2):
            pair = []
            for which, ref in enumerate((query_ref, grad_ref)):
                if block == 0:
                    start = pl.multiple_of(first_col + group * WIDE, WIDE)
                    source = ref.at[:, pl.ds(start, WIDE)]
                else:
                    source = partner_ref.at[:, pl.ds(which * HALF_Q + group * WIDE, WIDE)]
                pair.append(
                    pltpu.make_async_copy(
                        source,
                        rows_in.at[block, which, :, pl.ds(group * WIDE, WIDE)],
                        arrived.at[group, levels + 2 * block + which],
                    )
                )
            blocks.append(pair)
        arrivals.append((copies, blocks))
    for copies, blocks in arrivals:
        for copy in copies + blocks[0] + blocks[1]:
            copy.start()
    sums[...] = jnp.zeros_like(sums)

    key_at = lax.broadcasted_iota(jnp.int32, (BLOCK, BLOCK), 0)
    query_at = lax.broadcasted_iota(jnp.int32, (BLOCK, BLOCK), 1)
    told_list = told_ref[:, BLOCK : BLOCK + LIST + 1].astype(jnp.float32)
    lane = lax.broadcasted_iota(jnp.int32, told_list.shape, 1)

    def told_number(i):
        return jnp.sum(jnp.where(lane == i, told_list, 0.0)).astype(jnp.int32)

    shifts = []
    places = []
    for block in range(2):
        if block == 0:
            segs = segs_ref[...]
            listed = [list_ref[slot] for slot in range(LIST)]
            count = count_ref[0]
        else:
            segs = told_ref[:, :BLOCK]
            listed = [told_number(slot) for slot in range(LIST)]
            count = told_number(LIST)
        here = mine ^ block
        seg_of_query = jnp.broadcast_to(segs, (BLOCK, BLOCK))
        causal = (key_at <= query_at) & (seg_of_query.T == seg_of_query)
        bias[block] = jnp.where(causal, 0.0, MASKED)
        whole = [(slot < count) & (listed[slot] < here) for slot in range(LIST)]
        shifts.append([jnp.where(whole[slot], 0.0, -MASKED) for slot in range(1, LIST)])
        spots = []
        for slot in range(LIST):
            shown = jnp.where(whole[slot], listed[slot], here)
            spot = 2 * ((mine >> 1) - (shown >> 1)) + ((shown & 1) ^ side)
            spots.append(pl.ds(pl.multiple_of(spot * BLOCK, BLOCK), BLOCK))
        places.append(spots)

    departures = []

    def send(source, target):
        copy = pltpu.make_async_copy(source, target, left.at[len(departures)])
        copy.start()
        departures.append(copy)

    for group in range(HALF_KV):
        copies, blocks = arrivals[group]
        for copy in copies:
            copy.wait()
        key_cols = slice(group * PAIR, group * PAIR + HEAD_SIZE)
        value_cols = slice(group * PAIR + HEAD_SIZE, (group + 1) * PAIR)
        heads = [group * GROUP + h for h in range(GROUP)]
        for block in range(2):
            for copy in blocks[block]:
                copy.wait()

            def rows(which, head):
                return rows_in[block, which, :, head * HEAD_SIZE : (head + 1) * HEAD_SIZE]

            keys = jnp.concatenate([kv[at, key_cols] for at in places[block]], axis=0)
            values = jnp.concatenate([kv[at, value_cols] for at in places[block]], axis=0)
            shift = shifts[block]

            def products(h):
                query = jnp.concatenate([rows(0, heads[h]), rows(0, heads[h + 1])], axis=0)
                grad = jnp.concatenate([rows(1, heads[h]), rows(1, heads[h + 1])], axis=0)
                each = [slice(slot * BLOCK, (slot + 1) * BLOCK) for slot in range(LIST)]
                return (
                    [dot(keys[at], query, ((1,), (1,))) for at in each],
                    [dot(values[at], grad, ((1,), (1,))) for at in each],
                )

            for h in range(0, GROUP, 2):
                scores, dprobs = products(h)
                parts = list(scores)
                parts[0] = parts[0] + jnp.concatenate([bias[block], bias[block]], axis=1)

                def fold(value, by):
                    return by(value.reshape(BLOCK // 8, 8, 2 * BLOCK), axis=0)

                peak = fold(parts[0], jnp.max)
                for slot in range(1, LIST):
                    peak = jnp.maximum(peak, fold(parts[slot], jnp.max) - shift[slot - 1])
                peak = jnp.max(peak, axis=0, keepdims=True) * FACTOR
                peaks = [peak] + [peak + shift[slot - 1] for slot in range(1, LIST)]
                total = jnp.zeros((8, 2 * BLOCK), jnp.float32)
                mixed = jnp.zeros((8, 2 * BLOCK), jnp.float32)
                weights = []
                for slot in range(LIST):
                    weight = jnp.exp2(parts[slot] * FACTOR - peaks[slot])
                    total = total + fold(weight, jnp.sum)
                    mixed = mixed + fold(weight * dprobs[slot], jnp.sum)
                    weights.append(weight)
                inverse = 1.0 / jnp.sum(total, axis=0, keepdims=True)
                delta = jnp.sum(mixed, axis=0, keepdims=True) * inverse
                at = slice(h * BLOCK, (h + 2) * BLOCK)
                for slot in range(LIST):
                    full = weights[slot] * inverse
                    down = slice(slot * BLOCK, (slot + 1) * BLOCK)
                    probs[down, at] = full.astype(jnp.bfloat16)
                    dscores[down, at] = (full * (dprobs[slot] - delta)).astype(jnp.bfloat16)
            query_all = jnp.concatenate([rows(0, head) for head in heads], axis=0)
            grad_all = jnp.concatenate([rows(1, head) for head in heads], axis=0)
            query_grad = dot(dscores[...], keys, ((0,), (0,))) * SCALE
            for h, head in enumerate(heads):
                rows_out[block, :, head * HEAD_SIZE : (head + 1) * HEAD_SIZE] = query_grad[
                    h * BLOCK : (h + 1) * BLOCK
                ].astype(jnp.bfloat16)
            wide = pl.ds(group * WIDE, WIDE)
            send(rows_out.at[block, :, wide], outs[block].at[:, wide])
            key_terms = dot(dscores[...], query_all, ((1,), (0,))) * SCALE
            value_terms = dot(probs[...], grad_all, ((1,), (0,)))
            for slot in range(LIST):
                at = slice(slot * BLOCK, (slot + 1) * BLOCK)
                sums[places[block][slot], key_cols] += key_terms[at]
                sums[places[block][slot], value_cols] += value_terms[at]
        cols = slice(group * PAIR, (group + 1) * PAIR)
        for j in range(levels):
            terms[j][:, cols] = sums[rows_of[j], cols].astype(terms[j].dtype)
            cut = pl.ds(group * PAIR, PAIR)
            send(terms[j].at[:, cut], term_refs[j].at[:, cut])
    for copy in departures:
        copy.wait()


def attention(levels, lists, count, where, segs, told, queries, grads, partner, held):
    smem = pl.BlockSpec(memory_space=pltpu.SMEM)
    anywhere = pl.BlockSpec(memory_space=pl.ANY)
    keys = LIST * BLOCK
    width = HALF_KV * PAIR
    outs = [jax.ShapeDtypeStruct((BLOCK, HALF_Q), jnp.bfloat16)] * 2
    terms = [
        jax.ShapeDtypeStruct(
            (2 * BLOCK, width), jnp.bfloat16 if j in (1, levels - 1) else jnp.float32
        )
        for j in range(levels)
    ]
    return pl.pallas_call(
        lambda *refs: attention_kernel(levels, *refs),
        out_shape=outs + terms,
        in_specs=[smem, smem, smem, pl.BlockSpec(memory_space=pltpu.VMEM)] + [
            pl.BlockSpec(memory_space=pltpu.VMEM)
        ]
        + [anywhere] * (3 + levels),
        out_specs=[anywhere] * (2 + levels),
        scratch_shapes=[
            pltpu.VMEM((2 * levels * BLOCK, width), jnp.bfloat16),
            pltpu.VMEM((2, 2, BLOCK, HALF_Q), jnp.bfloat16),
            pltpu.VMEM((2, BLOCK, HALF_Q), jnp.bfloat16),
            pltpu.VMEM((2, BLOCK, BLOCK), jnp.float32),
            pltpu.VMEM((keys, WIDE), jnp.bfloat16),
            pltpu.VMEM((keys, WIDE), jnp.bfloat16),
            pltpu.VMEM((2 * levels * BLOCK, width), jnp.float32),
        ]
        + [pltpu.VMEM(term.shape, term.dtype) for term in terms]
        + [
            pltpu.SemaphoreType.DMA((HALF_KV, levels + 4)),
            pltpu.SemaphoreType.DMA((HALF_KV * (levels + 2),)),
        ],
        compiler_params=pltpu.CompilerParams(vmem_limit_bytes=60 * 1024 * 1024),
        cost_estimate=pl.CostEstimate(
            flops=5 * 2 * keys * HEAD_SIZE * BLOCK * QUERY_HEADS,
            bytes_accessed=8 * 1024 * 1024,
            transcendentals=keys * BLOCK * QUERY_HEADS,
        ),
    )(lists, count, where, segs, told, queries, grads, partner, *held[::-1])


def per_device(
    queries, key_heads, value_per_head, out_grads, segment_ids, block_lists, list_counts
):
    sections = lax.axis_size("section")
    blocks = lax.axis_size("blk")
    levels = blocks // 2
    mine = lax.axis_index("blk")
    side = mine % 2
    level = mine // 2
    swap = [(i, i ^ 1) for i in range(blocks)]

    def back(value, moved):
        pairs = [
            (s * blocks + b, (s - 1) % sections * blocks + moved(b))
            for s in range(sections)
            for b in range(blocks)
            if moved(b) >= 0
        ]
        return lax.ppermute(value, ("section", "blk"), pairs)

    def columns(array, start, width):
        return lax.dynamic_slice_in_dim(array[0], start, width, 1)

    def heads_of(half):
        parts = []
        for g in range(HALF_KV):
            start = half * KV_COLS + g * HEAD_SIZE
            parts += [columns(a, start, HEAD_SIZE) for a in (key_heads, value_per_head)]
        return jnp.concatenate(parts, axis=1)

    facts = jnp.concatenate([segment_ids[0], block_lists[0, 0], list_counts[0]])[None]
    told = lax.ppermute(facts, "blk", swap)
    other = lax.ppermute(heads_of(1 - side), "blk", swap)
    theirs = jnp.concatenate(
        [columns(a, (1 - side) * HALF_Q, HALF_Q) for a in (queries, out_grads)], axis=1
    )
    theirs, other = lax.optimization_barrier((theirs, other))
    partner = lax.ppermute(theirs, "blk", swap)
    held = [jnp.concatenate([heads_of(side), other], axis=0)]
    for hop in range(1, levels):
        pairs = [(i, i + 2 * hop) for i in range(blocks - 2 * hop)]
        held.append(lax.ppermute(held[0], "blk", pairs))

    top = levels - 1
    own_out, partner_out, here, near, *between, first = attention(
        levels,
        block_lists[0, 0],
        list_counts[0],
        jnp.stack([mine, jnp.where(level == top, top, 1)]).astype(jnp.int32),
        segment_ids,
        told,
        queries[0],
        out_grads[0],
        partner,
        held,
    )

    def down(terms, hop, lowest):
        pairs = [(i, i - 2 * hop) for i in range(2 * lowest, blocks)]
        return lax.ppermute(terms, "blk", pairs)

    landed = down(first, 1, 1)
    query_grads = (back(own_out, lambda b: b), back(partner_out, lambda b: b ^ 1))
    carried = landed
    for j in range(top - 1, 1, -1):
        total = between[j - 2] + carried.astype(jnp.float32)
        total = total.astype(jnp.bfloat16)
        carried = down(total, 1, j) if j > 2 else down(total, 2, 2)
    here = here + jnp.where(level == top - 1, 0.0, landed.astype(jnp.float32))
    near, here = lax.optimization_barrier((near, here))
    rest = down(near, 1, top)
    rest, query_grads, carried = lax.optimization_barrier((rest, query_grads, carried))
    totals = (here + carried.astype(jnp.float32) + rest.astype(jnp.float32)).astype(jnp.bfloat16)
    sums = [back(totals[:BLOCK], lambda b: b), back(totals[BLOCK:], lambda b: b ^ 1)]

    def ordered(a, b):
        return jnp.where(side == 0, jnp.concatenate([a, b], axis=1), jnp.concatenate([b, a], axis=1))

    grad_queries = ordered(*query_grads)

    def kind(total, which):
        starts = [g * PAIR + which * HEAD_SIZE for g in range(HALF_KV)]
        return jnp.concatenate([total[:, at : at + HEAD_SIZE] for at in starts], axis=1)

    grad_keys = ordered(kind(sums[0], 0), kind(sums[1], 0))
    grad_values = ordered(kind(sums[0], 1), kind(sums[1], 1))
    return (grad_queries[None], grad_keys[None], grad_values[None])


def solution(mesh):
    in_specs = (
        P("section", "blk", None),
        P("section", "blk", None),
        P("section", "blk", None),
        P("section", "blk", None),
        P("section", "blk"),
        P("section", "blk", None),
        P("section", "blk"),
    )
    out_specs = (P("section", "blk", None), P("section", "blk", None), P("section", "blk", None))
    return jax.shard_map(
        per_device, mesh=mesh, in_specs=in_specs, out_specs=out_specs, check_vma=False
    )
```

```python
import math

import jax
import jax.numpy as jnp
from jax import lax
from jax.experimental import pallas as pl
from jax.experimental.pallas import tpu as pltpu
from jax.sharding import PartitionSpec as P

QUERY_HEADS = 32
KEY_VALUE_HEADS = 4
HEAD_SIZE = 128
BLOCK = 128
LIST = 4
GROUP = QUERY_HEADS // KEY_VALUE_HEADS
HALF_KV = KEY_VALUE_HEADS // 2
HALF_Q = QUERY_HEADS // 2 * HEAD_SIZE
KV_COLS = HALF_KV * HEAD_SIZE
WIDE = GROUP * HEAD_SIZE
PAIR = 2 * HEAD_SIZE
MASKED = -1e30

SCALE = 1.0 / math.sqrt(HEAD_SIZE)
FACTOR = SCALE / math.log(2.0)


def dot(a, b, contract):
    return lax.dot_general(
        a, b, ((contract[0], contract[1]), ((), ())), preferred_element_type=jnp.float32
    )


def attention_kernel(levels, *refs):
    list_ref, count_ref, where_ref, segs_ref, told_ref = refs[:5]
    refs = refs[1:]
    query_ref, grad_ref, partner_ref = refs[4:7]
    held = refs[7 : 7 + levels][::-1]
    outs = refs[7 + levels : 9 + levels]
    term_refs = refs[9 + levels : 10 + 2 * levels]
    scratch = refs[10 + 2 * levels :]
    rows_of = [pl.ds(2 * j * BLOCK, 2 * BLOCK) for j in range(levels - 1)]
    rows_of.append(pl.ds(pl.multiple_of(2 * where_ref[1] * BLOCK, 2 * BLOCK), 2 * BLOCK))
    rows_of.append(rows_of[2])
    kv, rows_in, rows_out, bias, probs, dscores, sums = scratch[:7]
    terms = scratch[7 : 8 + levels]
    arrived, left = scratch[-2:]

    mine = where_ref[0]
    side = mine & 1
    first_col = side * HALF_Q
    arrivals = []
    for group in range(HALF_KV):
        at = pl.ds(group * PAIR, PAIR)
        copies = [
            pltpu.make_async_copy(
                held[j].at[:, at],
                kv.at[pl.ds(2 * j * BLOCK, 2 * BLOCK), at],
                arrived.at[group, j],
            )
            for j in range(levels)
        ]
        blocks = []
        for block in range(2):
            pair = []
            for which, ref in enumerate((query_ref, grad_ref)):
                if block == 0:
                    start = pl.multiple_of(first_col + group * WIDE, WIDE)
                    source = ref.at[:, pl.ds(start, WIDE)]
                else:
                    source = partner_ref.at[:, pl.ds(which * HALF_Q + group * WIDE, WIDE)]
                pair.append(
                    pltpu.make_async_copy(
                        source,
                        rows_in.at[block, which, :, pl.ds(group * WIDE, WIDE)],
                        arrived.at[group, levels + 2 * block + which],
                    )
                )
            blocks.append(pair)
        arrivals.append((copies, blocks))
    for copies, blocks in arrivals:
        for copy in copies + blocks[0] + blocks[1]:
            copy.start()
    sums[...] = jnp.zeros_like(sums)

    key_at = lax.broadcasted_iota(jnp.int32, (BLOCK, BLOCK), 0)
    query_at = lax.broadcasted_iota(jnp.int32, (BLOCK, BLOCK), 1)
    told_list = told_ref[:, BLOCK : BLOCK + LIST + 1].astype(jnp.float32)
    lane = lax.broadcasted_iota(jnp.int32, told_list.shape, 1)

    def told_number(i):
        return jnp.sum(jnp.where(lane == i, told_list, 0.0)).astype(jnp.int32)

    shifts = []
    places = []
    for block in range(2):
        if block == 0:
            segs = segs_ref[...]
            listed = [list_ref[slot] for slot in range(LIST)]
            count = count_ref[0]
        else:
            segs = told_ref[:, :BLOCK]
            listed = [told_number(slot) for slot in range(LIST)]
            count = told_number(LIST)
        here = mine ^ block
        seg_of_query = jnp.broadcast_to(segs, (BLOCK, BLOCK))
        causal = (key_at <= query_at) & (seg_of_query.T == seg_of_query)
        bias[block] = jnp.where(causal, 0.0, MASKED)
        whole = [(slot < count) & (listed[slot] < here) for slot in range(LIST)]
        shifts.append([jnp.where(whole[slot], 0.0, -MASKED) for slot in range(1, LIST)])
        spots = []
        for slot in range(LIST):
            shown = jnp.where(whole[slot], listed[slot], here)
            spot = 2 * ((mine >> 1) - (shown >> 1)) + ((shown & 1) ^ side)
            spots.append(pl.ds(pl.multiple_of(spot * BLOCK, BLOCK), BLOCK))
        places.append(spots)

    departures = []

    def send(source, target):
        copy = pltpu.make_async_copy(source, target, left.at[len(departures)])
        copy.start()
        departures.append(copy)

    for group in range(HALF_KV):
        copies, blocks = arrivals[group]
        for copy in copies:
            copy.wait()
        key_cols = slice(group * PAIR, group * PAIR + HEAD_SIZE)
        value_cols = slice(group * PAIR + HEAD_SIZE, (group + 1) * PAIR)
        heads = [group * GROUP + h for h in range(GROUP)]
        for block in range(2):
            for copy in blocks[block]:
                copy.wait()

            def rows(which, head):
                return rows_in[block, which, :, head * HEAD_SIZE : (head + 1) * HEAD_SIZE]

            keys = jnp.concatenate([kv[at, key_cols] for at in places[block]], axis=0)
            values = jnp.concatenate([kv[at, value_cols] for at in places[block]], axis=0)
            shift = shifts[block]

            def products(h):
                query = jnp.concatenate([rows(0, heads[h]), rows(0, heads[h + 1])], axis=0)
                grad = jnp.concatenate([rows(1, heads[h]), rows(1, heads[h + 1])], axis=0)
                each = [slice(slot * BLOCK, (slot + 1) * BLOCK) for slot in range(LIST)]
                return (
                    [dot(keys[at], query, ((1,), (1,))) for at in each],
                    [dot(values[at], grad, ((1,), (1,))) for at in each],
                )

            for h in range(0, GROUP, 2):
                scores, dprobs = products(h)
                parts = list(scores)
                parts[0] = parts[0] + jnp.concatenate([bias[block], bias[block]], axis=1)

                def fold(value, by):
                    return by(value.reshape(BLOCK // 8, 8, 2 * BLOCK), axis=0)

                peak = fold(parts[0], jnp.max)
                for slot in range(1, LIST):
                    peak = jnp.maximum(peak, fold(parts[slot], jnp.max) - shift[slot - 1])
                peak = jnp.max(peak, axis=0, keepdims=True) * FACTOR
                peaks = [peak] + [peak + shift[slot - 1] for slot in range(1, LIST)]
                total = jnp.zeros((8, 2 * BLOCK), jnp.float32)
                mixed = jnp.zeros((8, 2 * BLOCK), jnp.float32)
                weights = []
                for slot in range(LIST):
                    weight = jnp.exp2(parts[slot] * FACTOR - peaks[slot])
                    total = total + fold(weight, jnp.sum)
                    mixed = mixed + fold(weight * dprobs[slot], jnp.sum)
                    weights.append(weight)
                inverse = 1.0 / jnp.sum(total, axis=0, keepdims=True)
                delta = jnp.sum(mixed, axis=0, keepdims=True) * inverse
                at = slice(h * BLOCK, (h + 2) * BLOCK)
                for slot in range(LIST):
                    full = weights[slot] * inverse
                    down = slice(slot * BLOCK, (slot + 1) * BLOCK)
                    probs[down, at] = full.astype(jnp.bfloat16)
                    dscores[down, at] = (full * (dprobs[slot] - delta)).astype(jnp.bfloat16)
            query_all = jnp.concatenate([rows(0, head) for head in heads], axis=0)
            grad_all = jnp.concatenate([rows(1, head) for head in heads], axis=0)
            query_grad = dot(dscores[...], keys, ((0,), (0,))) * SCALE
            for h, head in enumerate(heads):
                rows_out[block, :, head * HEAD_SIZE : (head + 1) * HEAD_SIZE] = query_grad[
                    h * BLOCK : (h + 1) * BLOCK
                ].astype(jnp.bfloat16)
            wide = pl.ds(group * WIDE, WIDE)
            send(rows_out.at[block, :, wide], outs[block].at[:, wide])
            key_terms = dot(dscores[...], query_all, ((1,), (0,))) * SCALE
            value_terms = dot(probs[...], grad_all, ((1,), (0,)))
            for slot in range(LIST):
                at = slice(slot * BLOCK, (slot + 1) * BLOCK)
                sums[places[block][slot], key_cols] += key_terms[at]
                sums[places[block][slot], value_cols] += value_terms[at]
        cols = slice(group * PAIR, (group + 1) * PAIR)
        for j in range(levels + 1):
            terms[j][:, cols] = sums[rows_of[j], cols].astype(terms[j].dtype)
            cut = pl.ds(group * PAIR, PAIR)
            send(terms[j].at[:, cut], term_refs[j].at[:, cut])
    for copy in departures:
        copy.wait()


def attention(levels, lists, count, where, segs, told, queries, grads, partner, held):
    smem = pl.BlockSpec(memory_space=pltpu.SMEM)
    anywhere = pl.BlockSpec(memory_space=pl.ANY)
    keys = LIST * BLOCK
    width = HALF_KV * PAIR
    outs = [jax.ShapeDtypeStruct((BLOCK, HALF_Q), jnp.bfloat16)] * 2
    terms = [
        jax.ShapeDtypeStruct(
            (2 * BLOCK, width), jnp.bfloat16 if j in (1, levels - 1, levels) else jnp.float32
        )
        for j in range(levels + 1)
    ]
    return pl.pallas_call(
        lambda *refs: attention_kernel(levels, *refs),
        out_shape=outs + terms,
        in_specs=[smem, smem, smem, pl.BlockSpec(memory_space=pltpu.VMEM)] + [
            pl.BlockSpec(memory_space=pltpu.VMEM)
        ]
        + [anywhere] * (3 + levels),
        out_specs=[anywhere] * (3 + levels),
        scratch_shapes=[
            pltpu.VMEM((2 * levels * BLOCK, width), jnp.bfloat16),
            pltpu.VMEM((2, 2, BLOCK, HALF_Q), jnp.bfloat16),
            pltpu.VMEM((2, BLOCK, HALF_Q), jnp.bfloat16),
            pltpu.VMEM((2, BLOCK, BLOCK), jnp.float32),
            pltpu.VMEM((keys, WIDE), jnp.bfloat16),
            pltpu.VMEM((keys, WIDE), jnp.bfloat16),
            pltpu.VMEM((2 * levels * BLOCK, width), jnp.float32),
        ]
        + [pltpu.VMEM(term.shape, term.dtype) for term in terms]
        + [
            pltpu.SemaphoreType.DMA((HALF_KV, levels + 4)),
            pltpu.SemaphoreType.DMA((HALF_KV * (levels + 3),)),
        ],
        compiler_params=pltpu.CompilerParams(vmem_limit_bytes=60 * 1024 * 1024),
        cost_estimate=pl.CostEstimate(
            flops=5 * 2 * keys * HEAD_SIZE * BLOCK * QUERY_HEADS,
            bytes_accessed=8 * 1024 * 1024,
            transcendentals=keys * BLOCK * QUERY_HEADS,
        ),
    )(lists, count, where, segs, told, queries, grads, partner, *held[::-1])


def per_device(
    queries, key_heads, value_per_head, out_grads, segment_ids, block_lists, list_counts
):
    sections = lax.axis_size("section")
    blocks = lax.axis_size("blk")
    levels = blocks // 2
    mine = lax.axis_index("blk")
    side = mine % 2
    level = mine // 2
    swap = [(i, i ^ 1) for i in range(blocks)]

    def back(value, moved):
        pairs = [
            (s * blocks + b, (s - 1) % sections * blocks + moved(b))
            for s in range(sections)
            for b in range(blocks)
            if moved(b) >= 0
        ]
        return lax.ppermute(value, ("section", "blk"), pairs)

    def columns(array, start, width):
        return lax.dynamic_slice_in_dim(array[0], start, width, 1)

    def heads_of(half):
        parts = []
        for g in range(HALF_KV):
            start = half * KV_COLS + g * HEAD_SIZE
            parts += [columns(a, start, HEAD_SIZE) for a in (key_heads, value_per_head)]
        return jnp.concatenate(parts, axis=1)

    facts = jnp.concatenate([segment_ids[0], block_lists[0, 0], list_counts[0]])[None]
    told = lax.ppermute(facts, "blk", swap)
    other = lax.ppermute(heads_of(1 - side), "blk", swap)
    theirs = jnp.concatenate(
        [columns(a, (1 - side) * HALF_Q, HALF_Q) for a in (queries, out_grads)], axis=1
    )
    theirs, other = lax.optimization_barrier((theirs, other))
    partner = lax.ppermute(theirs, "blk", swap)
    held = [jnp.concatenate([heads_of(side), other], axis=0)]
    for hop in range(1, levels):
        pairs = [(i, i + 2 * hop) for i in range(blocks - 2 * hop)]
        held.append(lax.ppermute(held[0], "blk", pairs))

    top = levels - 1
    own_out, partner_out, here, near, *between, first, second = attention(
        levels,
        block_lists[0, 0],
        list_counts[0],
        jnp.stack([mine, jnp.where(level == top, top, 1)]).astype(jnp.int32),
        segment_ids,
        told,
        queries[0],
        out_grads[0],
        partner,
        held,
    )

    def down(terms, hop, levels_from):
        pairs = [(2 * z + p, 2 * (z - hop) + p) for z in levels_from for p in range(2)]
        return lax.ppermute(terms, "blk", pairs)

    landed = down(first, 1, range(1, levels))
    query_grads = (back(own_out, lambda b: b), back(partner_out, lambda b: b ^ 1))
    skipped = down(second, 2, [top])
    carried = landed
    for j in range(top - 1, 1, -1):
        total = between[j - 2] + carried.astype(jnp.float32)
        total = total.astype(jnp.bfloat16)
        if j == 2:
            near, total = lax.optimization_barrier((near, total))
        carried = down(total, 1, range(j, levels)) if j > 2 else down(total, 2, range(2, top))
    rest = down(near, 1, [top])
    here = here + jnp.where(level == top - 1, 0.0, landed.astype(jnp.float32))
    rest, skipped, query_grads, carried = lax.optimization_barrier(
        (rest, skipped, query_grads, carried)
    )
    for terms in (carried, skipped, rest):
        here = here + terms.astype(jnp.float32)
    totals = here.astype(jnp.bfloat16)
    sums = [back(totals[:BLOCK], lambda b: b), back(totals[BLOCK:], lambda b: b ^ 1)]

    def ordered(a, b):
        return jnp.where(side == 0, jnp.concatenate([a, b], axis=1), jnp.concatenate([b, a], axis=1))

    grad_queries = ordered(*query_grads)

    def kind(total, which):
        starts = [g * PAIR + which * HEAD_SIZE for g in range(HALF_KV)]
        return jnp.concatenate([total[:, at : at + HEAD_SIZE] for at in starts], axis=1)

    grad_keys = ordered(kind(sums[0], 0), kind(sums[1], 0))
    grad_values = ordered(kind(sums[0], 1), kind(sums[1], 1))
    return (grad_queries[None], grad_keys[None], grad_values[None])


def solution(mesh):
    in_specs = (
        P("section", "blk", None),
        P("section", "blk", None),
        P("section", "blk", None),
        P("section", "blk", None),
        P("section", "blk"),
        P("section", "blk", None),
        P("section", "blk"),
    )
    out_specs = (P("section", "blk", None), P("section", "blk", None), P("section", "blk", None))
    return jax.shard_map(
        per_device, mesh=mesh, in_specs=in_specs, out_specs=out_specs, check_vma=False
    )
```

```python
import math

import jax
import jax.numpy as jnp
from jax import lax
from jax.experimental import pallas as pl
from jax.experimental.pallas import tpu as pltpu
from jax.sharding import PartitionSpec as P

QUERY_HEADS = 32
KEY_VALUE_HEADS = 4
HEAD_SIZE = 128
BLOCK = 128
LIST = 4
GROUP = QUERY_HEADS // KEY_VALUE_HEADS
HALF_KV = KEY_VALUE_HEADS // 2
HALF_Q = QUERY_HEADS // 2 * HEAD_SIZE
KV_COLS = HALF_KV * HEAD_SIZE
WIDE = GROUP * HEAD_SIZE
PAIR = 2 * HEAD_SIZE
MASKED = -1e30

SCALE = 1.0 / math.sqrt(HEAD_SIZE)
FACTOR = SCALE / math.log(2.0)


def dot(a, b, contract):
    return lax.dot_general(
        a, b, ((contract[0], contract[1]), ((), ())), preferred_element_type=jnp.float32
    )


def attention_kernel(levels, *refs):
    list_ref, count_ref, where_ref, segs_ref, told_ref = refs[:5]
    refs = refs[1:]
    query_ref, grad_ref, partner_ref = refs[4:7]
    held = refs[7 : 7 + levels][::-1]
    outs = refs[7 + levels : 9 + levels]
    term_refs = refs[9 + levels : 9 + 2 * levels]
    scratch = refs[9 + 2 * levels :]
    rows_of = [pl.ds(2 * j * BLOCK, 2 * BLOCK) for j in range(levels - 1)]
    rows_of.append(pl.ds(pl.multiple_of(2 * where_ref[1] * BLOCK, 2 * BLOCK), 2 * BLOCK))
    kv, rows_in, rows_out, bias, probs, dscores, sums = scratch[:7]
    terms = scratch[7 : 7 + levels]
    arrived, left = scratch[-2:]

    mine = where_ref[0]
    side = mine & 1
    first_col = side * HALF_Q
    arrivals = []
    for group in range(HALF_KV):
        at = pl.ds(group * PAIR, PAIR)
        copies = [
            pltpu.make_async_copy(
                held[j].at[:, at],
                kv.at[pl.ds(2 * j * BLOCK, 2 * BLOCK), at],
                arrived.at[group, j],
            )
            for j in range(levels)
        ]
        blocks = []
        for block in range(2):
            pair = []
            for which, ref in enumerate((query_ref, grad_ref)):
                if block == 0:
                    start = pl.multiple_of(first_col + group * WIDE, WIDE)
                    source = ref.at[:, pl.ds(start, WIDE)]
                else:
                    source = partner_ref.at[:, pl.ds(which * HALF_Q + group * WIDE, WIDE)]
                pair.append(
                    pltpu.make_async_copy(
                        source,
                        rows_in.at[block, which, :, pl.ds(group * WIDE, WIDE)],
                        arrived.at[group, levels + 2 * block + which],
                    )
                )
            blocks.append(pair)
        arrivals.append((copies, blocks))
    for copies, blocks in arrivals:
        for copy in copies + blocks[0] + blocks[1]:
            copy.start()
    sums[...] = jnp.zeros_like(sums)

    key_at = lax.broadcasted_iota(jnp.int32, (BLOCK, BLOCK), 0)
    query_at = lax.broadcasted_iota(jnp.int32, (BLOCK, BLOCK), 1)
    told_list = told_ref[:, BLOCK : BLOCK + LIST + 1].astype(jnp.float32)
    lane = lax.broadcasted_iota(jnp.int32, told_list.shape, 1)

    def told_number(i):
        return jnp.sum(jnp.where(lane == i, told_list, 0.0)).astype(jnp.int32)

    shifts = []
    places = []
    for block in range(2):
        if block == 0:
            segs = segs_ref[...]
            listed = [list_ref[slot] for slot in range(LIST)]
            count = count_ref[0]
        else:
            segs = told_ref[:, :BLOCK]
            listed = [told_number(slot) for slot in range(LIST)]
            count = told_number(LIST)
        here = mine ^ block
        seg_of_query = jnp.broadcast_to(segs, (BLOCK, BLOCK))
        causal = (key_at <= query_at) & (seg_of_query.T == seg_of_query)
        bias[block] = jnp.where(causal, 0.0, MASKED)
        whole = [(slot < count) & (listed[slot] < here) for slot in range(LIST)]
        shifts.append([jnp.where(whole[slot], 0.0, -MASKED) for slot in range(1, LIST)])
        spots = []
        for slot in range(LIST):
            shown = jnp.where(whole[slot], listed[slot], here)
            spot = 2 * ((mine >> 1) - (shown >> 1)) + ((shown & 1) ^ side)
            spots.append(pl.ds(pl.multiple_of(spot * BLOCK, BLOCK), BLOCK))
        places.append(spots)

    departures = []

    def send(source, target):
        copy = pltpu.make_async_copy(source, target, left.at[len(departures)])
        copy.start()
        departures.append(copy)

    for group in range(HALF_KV):
        copies, blocks = arrivals[group]
        for copy in copies:
            copy.wait()
        key_cols = slice(group * PAIR, group * PAIR + HEAD_SIZE)
        value_cols = slice(group * PAIR + HEAD_SIZE, (group + 1) * PAIR)
        heads = [group * GROUP + h for h in range(GROUP)]
        for block in range(2):
            for copy in blocks[block]:
                copy.wait()

            def rows(which, head):
                return rows_in[block, which, :, head * HEAD_SIZE : (head + 1) * HEAD_SIZE]

            keys = jnp.concatenate([kv[at, key_cols] for at in places[block]], axis=0)
            values = jnp.concatenate([kv[at, value_cols] for at in places[block]], axis=0)
            shift = shifts[block]

            def products(h):
                query = jnp.concatenate([rows(0, heads[h]), rows(0, heads[h + 1])], axis=0)
                grad = jnp.concatenate([rows(1, heads[h]), rows(1, heads[h + 1])], axis=0)
                each = [slice(slot * BLOCK, (slot + 1) * BLOCK) for slot in range(LIST)]
                return (
                    [dot(keys[at], query, ((1,), (1,))) for at in each],
                    [dot(values[at], grad, ((1,), (1,))) for at in each],
                )

            for h in range(0, GROUP, 2):
                scores, dprobs = products(h)
                parts = list(scores)
                parts[0] = parts[0] + jnp.concatenate([bias[block], bias[block]], axis=1)

                def fold(value, by):
                    return by(value.reshape(BLOCK // 8, 8, 2 * BLOCK), axis=0)

                peak = fold(parts[0], jnp.max)
                for slot in range(1, LIST):
                    peak = jnp.maximum(peak, fold(parts[slot], jnp.max) - shift[slot - 1])
                peak = jnp.max(peak, axis=0, keepdims=True) * FACTOR
                peaks = [peak] + [peak + shift[slot - 1] for slot in range(1, LIST)]
                total = jnp.zeros((8, 2 * BLOCK), jnp.float32)
                mixed = jnp.zeros((8, 2 * BLOCK), jnp.float32)
                weights = []
                for slot in range(LIST):
                    weight = jnp.exp2(parts[slot] * FACTOR - peaks[slot])
                    total = total + fold(weight, jnp.sum)
                    mixed = mixed + fold(weight * dprobs[slot], jnp.sum)
                    weights.append(weight)
                inverse = 1.0 / jnp.sum(total, axis=0, keepdims=True)
                delta = jnp.sum(mixed, axis=0, keepdims=True) * inverse
                at = slice(h * BLOCK, (h + 2) * BLOCK)
                for slot in range(LIST):
                    full = weights[slot] * inverse
                    down = slice(slot * BLOCK, (slot + 1) * BLOCK)
                    probs[down, at] = full.astype(jnp.bfloat16)
                    dscores[down, at] = (full * (dprobs[slot] - delta)).astype(jnp.bfloat16)
            query_all = jnp.concatenate([rows(0, head) for head in heads], axis=0)
            grad_all = jnp.concatenate([rows(1, head) for head in heads], axis=0)
            query_grad = dot(dscores[...], keys, ((0,), (0,))) * SCALE
            for h, head in enumerate(heads):
                rows_out[block, :, head * HEAD_SIZE : (head + 1) * HEAD_SIZE] = query_grad[
                    h * BLOCK : (h + 1) * BLOCK
                ].astype(jnp.bfloat16)
            wide = pl.ds(group * WIDE, WIDE)
            send(rows_out.at[block, :, wide], outs[block].at[:, wide])
            key_terms = dot(dscores[...], query_all, ((1,), (0,))) * SCALE
            value_terms = dot(probs[...], grad_all, ((1,), (0,)))
            for slot in range(LIST):
                at = slice(slot * BLOCK, (slot + 1) * BLOCK)
                sums[places[block][slot], key_cols] += key_terms[at]
                sums[places[block][slot], value_cols] += value_terms[at]
        cols = slice(group * PAIR, (group + 1) * PAIR)
        for j in range(levels):
            terms[j][:, cols] = sums[rows_of[j], cols].astype(terms[j].dtype)
            cut = pl.ds(group * PAIR, PAIR)
            send(terms[j].at[:, cut], term_refs[j].at[:, cut])
    for copy in departures:
        copy.wait()


def attention(levels, lists, count, where, segs, told, queries, grads, partner, held):
    smem = pl.BlockSpec(memory_space=pltpu.SMEM)
    anywhere = pl.BlockSpec(memory_space=pl.ANY)
    keys = LIST * BLOCK
    width = HALF_KV * PAIR
    outs = [jax.ShapeDtypeStruct((BLOCK, HALF_Q), jnp.bfloat16)] * 2
    terms = [
        jax.ShapeDtypeStruct(
            (2 * BLOCK, width), jnp.float32 if j == 0 else jnp.bfloat16
        )
        for j in range(levels)
    ]
    return pl.pallas_call(
        lambda *refs: attention_kernel(levels, *refs),
        out_shape=outs + terms,
        in_specs=[smem, smem, smem, pl.BlockSpec(memory_space=pltpu.VMEM)] + [
            pl.BlockSpec(memory_space=pltpu.VMEM)
        ]
        + [anywhere] * (3 + levels),
        out_specs=[anywhere] * (2 + levels),
        scratch_shapes=[
            pltpu.VMEM((2 * levels * BLOCK, width), jnp.bfloat16),
            pltpu.VMEM((2, 2, BLOCK, HALF_Q), jnp.bfloat16),
            pltpu.VMEM((2, BLOCK, HALF_Q), jnp.bfloat16),
            pltpu.VMEM((2, BLOCK, BLOCK), jnp.float32),
            pltpu.VMEM((keys, WIDE), jnp.bfloat16),
            pltpu.VMEM((keys, WIDE), jnp.bfloat16),
            pltpu.VMEM((2 * levels * BLOCK, width), jnp.float32),
        ]
        + [pltpu.VMEM(term.shape, term.dtype) for term in terms]
        + [
            pltpu.SemaphoreType.DMA((HALF_KV, levels + 4)),
            pltpu.SemaphoreType.DMA((HALF_KV * (levels + 2),)),
        ],
        compiler_params=pltpu.CompilerParams(vmem_limit_bytes=60 * 1024 * 1024),
        cost_estimate=pl.CostEstimate(
            flops=5 * 2 * keys * HEAD_SIZE * BLOCK * QUERY_HEADS,
            bytes_accessed=8 * 1024 * 1024,
            transcendentals=keys * BLOCK * QUERY_HEADS,
        ),
    )(lists, count, where, segs, told, queries, grads, partner, *held[::-1])


def per_device(
    queries, key_heads, value_per_head, out_grads, segment_ids, block_lists, list_counts
):
    sections = lax.axis_size("section")
    blocks = lax.axis_size("blk")
    levels = blocks // 2
    mine = lax.axis_index("blk")
    side = mine % 2
    level = mine // 2
    swap = [(i, i ^ 1) for i in range(blocks)]

    def back(value, moved):
        pairs = [
            (s * blocks + b, (s - 1) % sections * blocks + moved(b))
            for s in range(sections)
            for b in range(blocks)
            if moved(b) >= 0
        ]
        return lax.ppermute(value, ("section", "blk"), pairs)

    def columns(array, start, width):
        return lax.dynamic_slice_in_dim(array[0], start, width, 1)

    def heads_of(half):
        parts = []
        for g in range(HALF_KV):
            start = half * KV_COLS + g * HEAD_SIZE
            parts += [columns(a, start, HEAD_SIZE) for a in (key_heads, value_per_head)]
        return jnp.concatenate(parts, axis=1)

    facts = jnp.concatenate([segment_ids[0], block_lists[0, 0], list_counts[0]])[None]
    told = lax.ppermute(facts, "blk", swap)
    other = lax.ppermute(heads_of(1 - side), "blk", swap)
    theirs = jnp.concatenate(
        [columns(a, (1 - side) * HALF_Q, HALF_Q) for a in (queries, out_grads)], axis=1
    )
    theirs, other = lax.optimization_barrier((theirs, other))
    partner = lax.ppermute(theirs, "blk", swap)
    held = [jnp.concatenate([heads_of(side), other], axis=0)]
    for hop in range(1, levels):
        pairs = [(i, i + 2 * hop) for i in range(blocks - 2 * hop)]
        held.append(lax.ppermute(held[0], "blk", pairs))

    top = levels - 1
    own_out, partner_out, here, near, *between, first = attention(
        levels,
        block_lists[0, 0],
        list_counts[0],
        jnp.stack([mine, jnp.where(level == top, top, 1)]).astype(jnp.int32),
        segment_ids,
        told,
        queries[0],
        out_grads[0],
        partner,
        held,
    )

    def down(terms, hop, levels_from):
        pairs = [(2 * z + p, 2 * (z - hop) + p) for z in levels_from for p in range(2)]
        return lax.ppermute(terms, "blk", pairs)

    landed = down(first, 1, range(1, levels))
    query_grads = (back(own_out, lambda b: b), back(partner_out, lambda b: b ^ 1))
    skipped = down(between[0], 2, [top])
    carried = landed
    for j in range(top - 1, 1, -1):
        total = between[j - 2].astype(jnp.float32) + carried.astype(jnp.float32)
        total = total.astype(jnp.bfloat16)
        if j == 2:
            near, total = lax.optimization_barrier((near, total))
        carried = down(total, 1, range(j, levels)) if j > 2 else down(total, 2, range(2, top))
    rest = down(near, 1, [top])
    here = here + jnp.where(level == top - 1, 0.0, landed.astype(jnp.float32))
    rest, skipped, query_grads, carried = lax.optimization_barrier(
        (rest, skipped, query_grads, carried)
    )
    for terms in (carried, skipped, rest):
        here = here + terms.astype(jnp.float32)
    totals = here.astype(jnp.bfloat16)
    sums = [back(totals[:BLOCK], lambda b: b), back(totals[BLOCK:], lambda b: b ^ 1)]

    def ordered(a, b):
        return jnp.where(side == 0, jnp.concatenate([a, b], axis=1), jnp.concatenate([b, a], axis=1))

    grad_queries = ordered(*query_grads)

    def kind(total, which):
        starts = [g * PAIR + which * HEAD_SIZE for g in range(HALF_KV)]
        return jnp.concatenate([total[:, at : at + HEAD_SIZE] for at in starts], axis=1)

    grad_keys = ordered(kind(sums[0], 0), kind(sums[1], 0))
    grad_values = ordered(kind(sums[0], 1), kind(sums[1], 1))
    return (grad_queries[None], grad_keys[None], grad_values[None])


def solution(mesh):
    in_specs = (
        P("section", "blk", None),
        P("section", "blk", None),
        P("section", "blk", None),
        P("section", "blk", None),
        P("section", "blk"),
        P("section", "blk", None),
        P("section", "blk"),
    )
    out_specs = (P("section", "blk", None), P("section", "blk", None), P("section", "blk", None))
    return jax.shard_map(
        per_device, mesh=mesh, in_specs=in_specs, out_specs=out_specs, check_vma=False
    )
```
